32 devices in a mesh: tiles: 8 (over y, x, core), cols: 4 (over z).
Axes of the slice: x: 2, y: 2, z: 4, core: 2. Of those that a mesh axis runs over, the one named last changes fastest.
Arguments:
- front_diag: float32 [4096, 4096], P('tiles', 'cols'), as said below
- front_below: float32 [4096, 4096], P('tiles', 'cols'), may hold values from -2 to 2
- ancestor: float32 [4096, 4096], P('tiles', 'cols'), may hold values from -6 to 6
- owner_cols: int32 [4], replicated, may hold values from 0 to 3, each once
- rel: int32 [4096], replicated, may hold values from 0 to 4095, as said below
Outputs:
- factor_diag: float32 [4096, 4096], P('tiles', 'cols')
- factor_below: float32 [4096, 4096], P('tiles', 'cols')
- ancestor_out: float32 [4096, 4096], P('tiles', 'cols')
The draws below stay inside these ranges and needn't reach their ends.
Inputs may be any that keep to these rules, and one draw needn't show every extreme that they name: Within each aligned block of 512 entries, rel is a permutation of that block's own indices. `owner_cols`: each column tile appears exactly once. `front_diag`: the symmetric block defined by the lower triangle is positive definite.
All inputs are finite; a program needn't handle non-finite values.
Results may differ from the reference program's by a relative error of at most 0.000073.
Values sent between devices are 32-bit elements; how exact they have to be, the bound alone decides.
No kernel may reach another device: no remote copies, remote signals or barrier semaphores. Data moves between devices by JAX's collectives and lax.ppermute only.
A program may use at most 128 MiB of HBM per device.

```python
import jax
import jax.numpy as jnp
from jax import lax

W = 4096
PANELS = 2
S = 4096
ROWS = 512
N_COLS = 4


def draw_front_diag(key, part):
    factor_key = jax.random.fold_in(key, 11)
    generator = jax.random.normal(factor_key, (W, W), jnp.float32)
    gram_part = jnp.dot(generator, generator.T, precision=lax.Precision.HIGHEST, preferred_element_type=jnp.float32) / W
    identity = jnp.eye(W, dtype=jnp.float32)
    matrix = gram_part + identity
    return matrix.astype(jnp.float32)


def draw_rel(key, part):
    block_count = S // ROWS
    block_keys = jax.random.split(jax.random.fold_in(key, 21), block_count)
    orders = jax.vmap(lambda block_key: jax.random.permutation(block_key, ROWS))(block_keys)
    offsets = jnp.arange(block_count, dtype=jnp.int32)[:, None] * ROWS
    return (orders.astype(jnp.int32) + offsets).reshape(S).astype(jnp.int32)


def level_of(own_key, extent, cuts, smallest, top_value):
    def one(dim, blocks):
        draws = jax.random.uniform(jax.random.fold_in(jax.random.fold_in(own_key, 6), dim), (blocks,), jnp.float32, smallest / len(cuts), top_value / len(cuts))
        return jnp.repeat(jnp.exp(draws), extent[dim] // blocks).reshape((-1,) + (1,) * (len(extent) - dim - 1))

    gain = one(*cuts[0])
    for cut in cuts[1:]:
        gain = gain * one(*cut)
    return gain


def scatter_about(key, dims, deviation, most, cuts=(), held_as=jnp.bfloat16):
    level = level_of(key, dims, cuts, -0.22, 0.18) if cuts else 1.0
    array = jax.random.normal(key, dims, jnp.float32) * deviation * level
    return jnp.minimum(jnp.maximum(array, -most), most).astype(held_as)


def setup_inputs(seed: int = 0) -> dict:
    seeds = jax.random.split(jax.random.key(seed), 6)
    front_diag = draw_front_diag(jax.random.fold_in(seeds[5], 71), 0)
    front_below = scatter_about(seeds[1], (S, W), 0.125, 2.0, ((0, 8), (1, 4)), jnp.float32)
    ancestor = scatter_about(seeds[2], (S, S), 1.0, 6.0, ((0, 8), (1, 4)), jnp.float32)
    owner_cols = jax.random.permutation(seeds[3], N_COLS).astype(jnp.int32)
    rel = draw_rel(jax.random.fold_in(seeds[5], 71), 0)
    return dict(front_diag=front_diag, front_below=front_below, ancestor=ancestor, owner_cols=owner_cols, rel=rel)


def reference(front_diag, front_below, ancestor, owner_cols, rel):
    precise = lax.Precision.HIGHEST
    tile_width = W // N_COLS
    lead = PANELS * tile_width
    symmetric = jnp.tril(front_diag) + jnp.tril(front_diag, -1).T
    first_factor = jnp.linalg.cholesky(symmetric[:lead, :lead])
    side_factor = jax.scipy.linalg.solve_triangular(first_factor, symmetric[lead:, :lead].T, lower=True).T
    trailing = symmetric[lead:, lead:] - jnp.dot(side_factor.astype(jnp.float32), side_factor.T.astype(jnp.float32), precision=precise, preferred_element_type=jnp.float32)
    top_rows = jnp.concatenate([first_factor, jnp.zeros((lead, W - lead), jnp.float32)], 1)
    low_rows = jnp.concatenate([side_factor, jnp.tril(trailing)], 1)
    factor_diag = jnp.concatenate([top_rows, low_rows], 0)
    below_lead = jax.scipy.linalg.solve_triangular(first_factor, front_below[:, :lead].T, lower=True).T
    below_rest = front_below[:, lead:] - jnp.dot(below_lead.astype(jnp.float32), side_factor.T.astype(jnp.float32), precision=precise, preferred_element_type=jnp.float32)
    factor_below = jnp.concatenate([below_lead, below_rest], 1)
    update = jnp.dot(below_lead.astype(jnp.float32), below_lead.T.astype(jnp.float32), precision=precise, preferred_element_type=jnp.float32)
    inverse = jnp.zeros((N_COLS,), jnp.int32).at[owner_cols].set(jnp.arange(N_COLS, dtype=jnp.int32))
    positions = jnp.arange(S, dtype=jnp.int32)
    tile_of = positions // tile_width
    column_place = inverse[tile_of] * tile_width + rel - tile_of * tile_width
    placed = jnp.zeros((S, S), jnp.float32).at[rel].set(update)
    placed = jnp.zeros((S, S), jnp.float32).at[:, column_place].set(placed)
    return (factor_diag, factor_below, ancestor - placed)
```

```python
import functools

import jax
import jax.numpy as jnp
from jax import lax
from jax.experimental import pallas as pl
from jax.experimental.pallas import tpu as pltpu
from jax.sharding import PartitionSpec as P

PANELS = 2
BLOCK = 128
GROUP = 8


def factor_block(block):
    group_count = BLOCK // GROUP
    lane = lax.broadcasted_iota(jnp.int32, (GROUP, BLOCK), 1)
    sub = lax.broadcasted_iota(jnp.int32, (GROUP, BLOCK), 0)
    rows = [block[GROUP * m : GROUP * (m + 1), :] for m in range(group_count)]
    factor = [jnp.zeros((GROUP, BLOCK), jnp.float32) for _ in range(group_count)]
    inverse = []
    for s in range(group_count):
        first = GROUP * s
        columns = {
            m: [
                jnp.broadcast_to(rows[m][:, first + j : first + j + 1], (GROUP, BLOCK))
                for j in range(GROUP)
            ]
            for m in range(s, group_count)
        }
        entry = {
            (k, j): jnp.broadcast_to(columns[s][j][k : k + 1, :], (GROUP, BLOCK))
            for j in range(GROUP)
            for k in range(j, GROUP)
        }
        here = (lane >= first) & (lane < first + GROUP)
        own = jnp.where(here, (lane - first == sub).astype(jnp.float32), rows[s])
        spread = [jnp.broadcast_to(own[k : k + 1, :], (GROUP, BLOCK)) for k in range(GROUP)]
        reciprocal, ratio = [], {}
        for j in range(GROUP):
            reciprocal.append(1.0 / entry[j, j])
            for k in range(j + 1, GROUP):
                ratio[k, j] = entry[k, j] * reciprocal[j]
            for k in range(j + 1, GROUP):
                for i in range(k, GROUP):
                    entry[i, k] = entry[i, k] - entry[i, j] * ratio[k, j]
                spread[k] = spread[k] - ratio[k, j] * spread[j]
        scale = [lax.rsqrt(entry[j, j]) for j in range(GROUP)]
        for m in range(s, group_count):
            piece = columns[m]
            for k in range(GROUP):
                for j in range(k):
                    piece[k] = piece[k] - ratio[k, j] * piece[j]
                factor[m] = jnp.where(lane == first + k, piece[k] * scale[k], factor[m])
            if m > s:
                parts = [piece[k] * reciprocal[k] * spread[k] for k in range(GROUP)]
                while len(parts) > 1:
                    parts = [parts[i] + parts[i + 1] for i in range(0, len(parts), 2)]
                rows[m] = jnp.where(here, 0.0, rows[m]) - parts[0]
        done = jnp.zeros((GROUP, BLOCK), jnp.float32)
        for k in range(GROUP):
            done = jnp.where(sub == k, spread[k] * scale[k], done)
        inverse.append(jnp.where(lane <= first + sub, done, 0.0))
        factor[s] = jnp.where(lane <= first + sub, factor[s], 0.0)
    return jnp.concatenate(factor, 0), jnp.concatenate(inverse, 0)


def exact_dot(left, right, dims):
    return lax.dot_general(
        left, right, (dims, ((), ())),
        precision=lax.Precision.HIGHEST, preferred_element_type=jnp.float32,
    )


def factor_kernel(a_ref, l_ref, w_ref, s_ref):
    order = a_ref.shape[0]
    count = order // BLOCK
    row = lax.broadcasted_iota(jnp.int32, (BLOCK, BLOCK), 0)
    col = lax.broadcasted_iota(jnp.int32, (BLOCK, BLOCK), 1)
    for i in range(count):
        for j in range(i + 1):
            tile = a_ref[i * BLOCK : (i + 1) * BLOCK, j * BLOCK : (j + 1) * BLOCK]
            flipped = tile.T
            if i == j:
                tile = jnp.where(row >= col, tile, flipped)
            else:
                s_ref[j * BLOCK : (j + 1) * BLOCK, i * BLOCK : (i + 1) * BLOCK] = flipped
            s_ref[i * BLOCK : (i + 1) * BLOCK, j * BLOCK : (j + 1) * BLOCK] = tile
    l_ref[...] = jnp.zeros_like(l_ref)
    lane = lax.broadcasted_iota(jnp.int32, (BLOCK, order), 1)

    def step(b, carry):
        start = pl.multiple_of(b * BLOCK, BLOCK)
        own = pl.ds(start, BLOCK)
        lower, inverse = factor_block(s_ref[own, own])
        l_ref[own, own] = lower
        s_ref[own, own] = (row == col).astype(jnp.float32)
        strip = exact_dot(inverse, s_ref[own, :], ((1,), (0,)))
        w_ref[own, :] = jnp.where(lane < start + BLOCK, strip, 0.0)

        def below(m, carry):
            these = pl.ds(pl.multiple_of(m * BLOCK, BLOCK), BLOCK)
            solved = exact_dot(s_ref[these, own], inverse, ((1,), (1,)))
            l_ref[these, own] = solved
            s_ref[these, own] = jnp.zeros((BLOCK, BLOCK), jnp.float32)
            s_ref[these, :] = s_ref[these, :] - exact_dot(solved, strip, ((1,), (0,)))
            return carry

        return lax.fori_loop(b + 1, count, below, carry)

    lax.fori_loop(0, count, step, 0)


def factor_tile(tile):
    order = tile.shape[0]
    flat = jax.ShapeDtypeStruct((order, order), jnp.float32)
    return pl.pallas_call(
        factor_kernel,
        out_shape=[flat, flat],
        in_specs=[pl.BlockSpec(memory_space=pltpu.VMEM)],
        out_specs=[pl.BlockSpec(memory_space=pltpu.VMEM)] * 2,
        scratch_shapes=[pltpu.VMEM((order, order), jnp.float32)],
        compiler_params=pltpu.CompilerParams(vmem_limit_bytes=32 * 2**20),
        cost_estimate=pl.CostEstimate(
            flops=order * 60_000_000, transcendentals=0, bytes_accessed=12 * order * order
        ),
    )(tile)


def dot_nt(left, right):
    return lax.dot_general(
        left, right, (((1,), (1,)), ((), ())),
        precision=lax.Precision.HIGH, preferred_element_type=jnp.float32,
    )


def dot_nn(left, right):
    return lax.dot_general(
        left, right, (((1,), (0,)), ((), ())),
        precision=lax.Precision.HIGH, preferred_element_type=jnp.float32,
    )


def exchange(block, bit, tile_count):
    return lax.ppermute(block, "tiles", [(i, i ^ bit) for i in range(tile_count)])


def tile_bits(tile_count):
    bits, bit = [], 2
    while bit < tile_count:
        bits.append(bit)
        bit *= 2
    return bits + [1]


def along_cols(block, source, col_pos, col_count):
    out = block
    for step in (1, -1):
        held, at = block, source
        while 0 <= at + step < col_count:
            held = lax.ppermute(held, "cols", [(at, at + step)])
            at += step
            out = jnp.where(col_pos == at, held, out)
    return out


def gather_rows(piece, tile_pos, tile_count):
    held = piece[None]
    bits = tile_bits(tile_count)
    for bit in bits:
        held = jnp.concatenate((held, exchange(held, bit, tile_count)), 0)
    weights = []
    for m in range(tile_count):
        weights.append(sum(bit for p, bit in enumerate(bits) if m >> p & 1))
    place = {w: m for m, w in enumerate(weights)}
    sorted_pieces = []
    table = jnp.array([place[w] for w in range(tile_count)], jnp.int32)
    for i in range(tile_count):
        m = table[i ^ tile_pos]
        sorted_pieces.append(lax.dynamic_index_in_dim(held, m, 0, keepdims=False))
    return jnp.concatenate(sorted_pieces, 1)


def fetch_target(block, tile_pos, tile_count, target):
    for bit in tile_bits(tile_count)[:-1]:
        other = exchange(block, bit, tile_count)
        mine = (tile_pos & bit) == ((2 * target) & bit)
        block = jnp.where(mine, block, other)
    other = exchange(block, 1, tile_count)
    even = tile_pos % 2 == 0
    return jnp.concatenate((jnp.where(even, block, other), jnp.where(even, other, block)), 0)


def shards(tile_count, col_count, front_diag, front_below, ancestor, owner_cols, rel):
    rows, width = front_diag.shape
    lead = PANELS * width
    steps = lead // rows
    tile_pos = lax.axis_index("tiles")
    col_pos = lax.axis_index("cols")
    target = lax.dynamic_slice_in_dim(owner_cols, col_pos, 1)[0]
    later_col = jnp.maximum(col_pos, PANELS)

    pieces = lax.all_to_all(
        front_diag.reshape(tile_count, rows // tile_count, width), "tiles", 0, 0, tiled=True
    )

    def spread_pieces(first, count, columns):
        parts = []
        for panel in range(PANELS):
            take = min(width, columns - panel * width)
            if take > 0:
                parts.append(
                    along_cols(
                        pieces[first : first + count, :, :take], panel, col_pos, col_count
                    )
                )
        return jnp.concatenate(parts, 2)

    lead_rows = []
    for i in range(steps):
        piece = spread_pieces(i, 1, (i + 1) * rows)
        lead_rows.append(gather_rows(piece, tile_pos, tile_count)[0])
    own_below = jnp.concatenate(
        [along_cols(front_below, panel, col_pos, col_count) for panel in range(PANELS)], 1
    )
    side = gather_rows(
        spread_pieces(steps, tile_count - steps, lead), tile_pos, tile_count
    )
    target_below = fetch_target(own_below, tile_pos, tile_count, target)
    match_side = lax.dynamic_slice_in_dim(side, 2 * later_col - steps, 2, 0).reshape(width, lead)
    own_side = lax.dynamic_index_in_dim(
        side, jnp.maximum(tile_pos - steps, 0), 0, keepdims=False
    )

    factor_rows, inverse_rows = [], []
    for i in range(steps):
        diag = lead_rows[i][:, i * rows :]
        if i:
            front = lead_rows[i][:, : i * rows]
            solved = jnp.concatenate(
                [
                    dot_nt(front[:, : (j + 1) * rows], inverse_rows[j][:, : (j + 1) * rows])
                    for j in range(i)
                ],
                1,
            )
            diag = diag - dot_nt(solved, solved)
        factor, inverse = factor_tile(diag)
        if i:
            done = jnp.concatenate(inverse_rows, 0)[:, : i * rows]
            cross = -dot_nn(inverse, dot_nn(solved, done))
            factor_row = jnp.concatenate((solved, factor), 1)
            inverse_row = jnp.concatenate((cross, inverse), 1)
        else:
            factor_row, inverse_row = factor, inverse
        fill = ((0, 0), (0, lead - (i + 1) * rows))
        factor_rows.append(jnp.pad(factor_row, fill))
        inverse_rows.append(jnp.pad(inverse_row, fill))
    both = jnp.concatenate((own_below, own_side), 0)
    solved = jnp.concatenate(
        [
            dot_nt(both[:, : (j + 1) * rows], inverse_rows[j][:, : (j + 1) * rows])
            for j in range(steps)
        ],
        1,
    )
    full_inverse = jnp.concatenate(inverse_rows, 0)
    again = jnp.concatenate(
        [
            dot_nn(
                solved[:, j * rows :], full_inverse[j * rows :, j * rows : (j + 1) * rows]
            )
            for j in range(steps)
        ],
        1,
    )
    change = dot_nt(again, match_side)
    panel_col = jnp.minimum(col_pos, PANELS - 1) * width
    own_solved = lax.dynamic_slice_in_dim(solved, panel_col, width, 1)
    in_lead = col_pos < PANELS
    factor_below = jnp.where(in_lead, own_solved[:rows], front_below - change[:rows])
    lead_factor = lax.dynamic_slice(
        jnp.concatenate(factor_rows, 0),
        (jnp.minimum(tile_pos, steps - 1) * rows, panel_col),
        (rows, width),
    )
    lead_part = jnp.where(tile_pos < steps, lead_factor, own_solved[rows:])
    global_rows = tile_pos * rows + jnp.arange(rows, dtype=jnp.int32)
    global_cols = col_pos * width + jnp.arange(width, dtype=jnp.int32)
    lower_mask = global_rows[:, None] >= global_cols[None, :]
    factor_diag = jnp.where(
        lower_mask, jnp.where(in_lead, lead_part, front_diag - change[rows:]), 0.0
    )
    update = dot_nt(again[:rows], target_below)
    row_places = lax.dynamic_slice_in_dim(rel, tile_pos * rows, rows) - tile_pos * rows
    row_move = (row_places[None, :] == jnp.arange(rows, dtype=jnp.int32)[:, None]).astype(
        jnp.float32
    )
    moved = dot_nn(row_move, update)
    parts = []
    for half in range(width // rows):
        start = target * width + half * rows
        places = lax.dynamic_slice_in_dim(rel, start, rows) - start
        move = (places[None, :] == jnp.arange(rows, dtype=jnp.int32)[:, None]).astype(
            jnp.float32
        )
        parts.append(dot_nt(moved[:, half * rows : (half + 1) * rows], move))
    return (factor_diag, factor_below, ancestor - jnp.concatenate(parts, 1))


def solution(mesh):
    placed = (P("tiles", "cols"), P("tiles", "cols"), P("tiles", "cols"), P(), P())
    return jax.shard_map(
        functools.partial(shards, mesh.shape["tiles"], mesh.shape["cols"]),
        mesh=mesh,
        in_specs=placed,
        out_specs=(P("tiles", "cols"), P("tiles", "cols"), P("tiles", "cols")),
        check_vma=False,
    )
```

```python
import functools

import jax
import jax.numpy as jnp
from jax import lax
from jax.experimental import pallas as pl
from jax.experimental.pallas import tpu as pltpu
from jax.sharding import PartitionSpec as P

PANELS = 2
BLOCK = 128
GROUP = 8


def factor_block(block):
    group_count = BLOCK // GROUP
    lane = lax.broadcasted_iota(jnp.int32, (GROUP, BLOCK), 1)
    sub = lax.broadcasted_iota(jnp.int32, (GROUP, BLOCK), 0)
    rows = [block[GROUP * m : GROUP * (m + 1), :] for m in range(group_count)]
    factor = [jnp.zeros((GROUP, BLOCK), jnp.float32) for _ in range(group_count)]
    inverse = []
    for s in range(group_count):
        first = GROUP * s
        columns = {
            m: [
                jnp.broadcast_to(rows[m][:, first + j : first + j + 1], (GROUP, BLOCK))
                for j in range(GROUP)
            ]
            for m in range(s, group_count)
        }
        entry = {
            (k, j): jnp.broadcast_to(columns[s][j][k : k + 1, :], (GROUP, BLOCK))
            for j in range(GROUP)
            for k in range(j, GROUP)
        }
        here = (lane >= first) & (lane < first + GROUP)
        own = jnp.where(here, (lane - first == sub).astype(jnp.float32), rows[s])
        spread = [jnp.broadcast_to(own[k : k + 1, :], (GROUP, BLOCK)) for k in range(GROUP)]
        reciprocal, ratio = [], {}
        for j in range(GROUP):
            reciprocal.append(1.0 / entry[j, j])
            for k in range(j + 1, GROUP):
                ratio[k, j] = entry[k, j] * reciprocal[j]
            for k in range(j + 1, GROUP):
                for i in range(k, GROUP):
                    entry[i, k] = entry[i, k] - entry[i, j] * ratio[k, j]
                spread[k] = spread[k] - ratio[k, j] * spread[j]
        scale = [lax.rsqrt(entry[j, j]) for j in range(GROUP)]
        for m in range(s, group_count):
            piece = columns[m]
            for k in range(GROUP):
                for j in range(k):
                    piece[k] = piece[k] - ratio[k, j] * piece[j]
                factor[m] = jnp.where(lane == first + k, piece[k] * scale[k], factor[m])
            if m > s:
                parts = [piece[k] * reciprocal[k] * spread[k] for k in range(GROUP)]
                while len(parts) > 1:
                    parts = [parts[i] + parts[i + 1] for i in range(0, len(parts), 2)]
                rows[m] = jnp.where(here, 0.0, rows[m]) - parts[0]
        done = jnp.zeros((GROUP, BLOCK), jnp.float32)
        for k in range(GROUP):
            done = jnp.where(sub == k, spread[k] * scale[k], done)
        inverse.append(jnp.where(lane <= first + sub, done, 0.0))
        factor[s] = jnp.where(lane <= first + sub, factor[s], 0.0)
    return jnp.concatenate(factor, 0), jnp.concatenate(inverse, 0)


def exact_dot(left, right, dims):
    return lax.dot_general(
        left, right, (dims, ((), ())),
        precision=lax.Precision.HIGHEST, preferred_element_type=jnp.float32,
    )


def split(value):
    high = value.astype(jnp.bfloat16)
    return high, (value - high.astype(jnp.float32)).astype(jnp.bfloat16)


NT = ((1,), (1,))
NN = ((1,), (0,))


def dot3(left, right, dims):
    def one(a, b):
        return lax.dot_general(a, b, (dims, ((), ())), preferred_element_type=jnp.float32)

    return one(left[0], right[0]) + (one(left[0], right[1]) + one(left[1], right[0]))


def columns_of(pair, start, stop):
    return pair[0][:, start:stop], pair[1][:, start:stop]


def collect(held_ref, chosen, out_ref, tile_pos, order, sems):
    count, rows = held_ref.shape[0], held_ref.shape[2]
    copies = []
    for i in range(count):
        place = 0
        if count > 1:
            apart = i ^ tile_pos
            for p, bit in enumerate(order):
                place = place + ((apart // bit) % 2) * 2**p
        copies.append(
            pltpu.make_async_copy(
                held_ref.at[place, chosen], out_ref.at[pl.ds(i * rows, rows), :], sems.at[i]
            )
        )
    return copies


def tile_kernel(index, first, last, order, waits, *refs):
    refs = list(refs)
    begin = first == 0
    if begin:
        info_ref, held_ref = refs.pop(0), refs.pop(0)
    else:
        state = [refs.pop(0) for _ in range(3)]
    done_refs = [(refs.pop(0), refs.pop(0)) for _ in range(index)]
    del refs[:waits]
    l_ref, w_ref, s_ref, high_ref, low_ref, token_ref = refs[:6]
    token_ref[0, 0] = 0.0
    rows = s_ref.shape[0]
    count = rows // BLOCK
    lead = index * rows
    row = lax.broadcasted_iota(jnp.int32, (BLOCK, BLOCK), 0)
    col = lax.broadcasted_iota(jnp.int32, (BLOCK, BLOCK), 1)
    if begin:
        t_ref, sems = refs[6:]
        copies = collect(held_ref, 0, t_ref, info_ref[0], order, sems)
        for copy in copies:
            copy.start()
        l_ref[:, lead:] = jnp.zeros((rows, rows), jnp.float32)
        w_ref[...] = jnp.zeros_like(w_ref)
        for copy in copies:
            copy.wait()
        diag = t_ref[:, lead:]
        if index:
            given = split(t_ref[:, :lead])
            for j in range(index):
                end = (j + 1) * rows
                pair = done_refs[j][0][...], done_refs[j][1][...]
                l_ref[:, j * rows : end] = dot3(columns_of(given, 0, end), pair, NT)
            solved = split(l_ref[:, :lead])
            diag = diag - dot3(solved, solved, NT)
        for i in range(count):
            for j in range(i + 1):
                tile = diag[i * BLOCK : (i + 1) * BLOCK, j * BLOCK : (j + 1) * BLOCK]
                flipped = tile.T
                if i == j:
                    tile = jnp.where(row >= col, tile, flipped)
                else:
                    s_ref[j * BLOCK : (j + 1) * BLOCK, i * BLOCK : (i + 1) * BLOCK] = flipped
                s_ref[i * BLOCK : (i + 1) * BLOCK, j * BLOCK : (j + 1) * BLOCK] = tile
    else:
        for source, target in zip(state, (l_ref, w_ref, s_ref)):
            target[...] = source[...]
    lane = lax.broadcasted_iota(jnp.int32, (BLOCK, rows), 1)

    def step(b, carry):
        start = pl.multiple_of(b * BLOCK, BLOCK)
        own = pl.ds(start, BLOCK)
        own_l = pl.ds(pl.multiple_of(lead + b * BLOCK, BLOCK), BLOCK)
        lower, inverse = factor_block(s_ref[own, own])
        l_ref[own, own_l] = lower
        s_ref[own, own] = (row == col).astype(jnp.float32)
        strip = exact_dot(inverse, s_ref[own, :], NN)
        w_ref[own, :] = jnp.where(lane < start + BLOCK, strip, 0.0)

        def below(m, carry):
            these = pl.ds(pl.multiple_of(m * BLOCK, BLOCK), BLOCK)
            solved = exact_dot(s_ref[these, own], inverse, NT)
            l_ref[these, own_l] = solved
            s_ref[these, own] = jnp.zeros((BLOCK, BLOCK), jnp.float32)
            s_ref[these, :] = s_ref[these, :] - exact_dot(solved, strip, NN)
            return carry

        return lax.fori_loop(b + 1, count, below, carry)

    lax.fori_loop(first, last, step, 0)
    if last == count:
        inverse = split(w_ref[...])
        high_ref[:, lead:], low_ref[:, lead:] = inverse
        if index:
            solved = split(l_ref[:, :lead])
            for k in range(index):
                total = None
                for j in range(k, index):
                    pair = columns_of(done_refs[j], k * rows, (k + 1) * rows)
                    term = dot3(columns_of(solved, j * rows, (j + 1) * rows), pair, NN)
                    total = term if total is None else total + term
                cross = split(-dot3(inverse, split(total), NN))
                here = slice(k * rows, (k + 1) * rows)
                high_ref[:, here], low_ref[:, here] = cross


VMEM = pl.BlockSpec(memory_space=pltpu.VMEM)
SMEM = pl.BlockSpec(memory_space=pltpu.SMEM)
ANY = pl.BlockSpec(memory_space=pl.ANY)


def limit(size=60):
    return pltpu.CompilerParams(vmem_limit_bytes=size * 2**20)


def cost(flops):
    return pl.CostEstimate(flops=flops, transcendentals=0, bytes_accessed=2**20)


TOKEN = jax.ShapeDtypeStruct((1, 1), jnp.float32)


def tile_part(index, first, last, rows, order, info, held, state, done, waits):
    flat = jax.ShapeDtypeStruct((rows, rows), jnp.float32)
    wide = jax.ShapeDtypeStruct((rows, (index + 1) * rows), jnp.float32)
    half = jax.ShapeDtypeStruct((rows, (index + 1) * rows), jnp.bfloat16)
    begin = first == 0
    given = [info, held] if begin else list(state)
    pairs = [part for pair in done for part in pair]
    return pl.pallas_call(
        functools.partial(tile_kernel, index, first, last, order, len(waits)),
        out_shape=[wide, flat, flat, half, half, TOKEN],
        in_specs=([SMEM, ANY] if begin else [VMEM] * 3) + [VMEM] * len(pairs) + [ANY] * len(waits),
        out_specs=[VMEM] * 5 + [SMEM],
        scratch_shapes=[
            pltpu.VMEM((rows, (index + 1) * rows), jnp.float32),
            pltpu.SemaphoreType.DMA((held.shape[0],)),
        ] if begin else [],
        compiler_params=limit(),
        cost_estimate=cost((last - first) * 8_000_000_000),
    )(*given, *pairs, *waits)


def both_solves(source, width, panel, inverse, solved_ref, scratch_ref, high_ref, low_ref):
    rows = source[0].shape[0]
    steps = len(inverse)
    step = inverse[0][0].shape[0]
    for j in range(steps):
        pair = inverse[j][0][...], inverse[j][1][...]
        scratch_ref[:, j * step : (j + 1) * step] = dot3(
            columns_of(source, 0, (j + 1) * step), pair, NT
        )
    solved_ref[...] = jnp.where(panel == 0, scratch_ref[:, :width], scratch_ref[:, width:])
    solved = split(scratch_ref[...])
    for k in range(steps):
        total = None
        for j in range(k, steps):
            pair = columns_of(inverse[j], k * step, (k + 1) * step)
            term = dot3(columns_of(solved, j * step, (j + 1) * step), pair, NN)
            total = term if total is None else total + term
        here = slice(k * step, (k + 1) * step)
        high_ref[:, here], low_ref[:, here] = split(total)


def below_kernel(steps, info_ref, *refs):
    refs = list(refs)
    held = [(refs.pop(0), refs.pop(0)) for _ in range(CHUNKS)]
    inverse = [(refs.pop(0), refs.pop(0)) for _ in range(steps)]
    solved_ref, high_ref, low_ref, token_ref, scratch_ref = refs
    token_ref[0, 0] = 0.0
    width = solved_ref.shape[1]
    chunk = width // CHUNKS
    even = info_ref[1] % 2 == 0
    for k, (own, other) in enumerate(held):
        for panel in range(PANELS):
            start = panel * width + k * chunk
            pick = even if panel == 0 else jnp.logical_not(even)
            scratch_ref[:, start : start + chunk] = jnp.where(pick, own[...], other[...])
    both_solves(
        split(scratch_ref[...]), width, info_ref[1], inverse, solved_ref, scratch_ref, high_ref, low_ref
    )


def side_kernel(orders, steps, sizes, info_ref, *refs):
    refs = list(refs)
    held = [refs.pop(0) for _ in sizes]
    inverse = [(refs.pop(0), refs.pop(0)) for _ in range(steps)]
    solved_ref, high_ref, low_ref, token_ref, scratch_ref, sems = refs
    token_ref[0, 0] = 0.0
    tile_pos = info_ref[0]
    own = jnp.maximum(tile_pos - steps, 0)
    start = 0
    for ref, size, order in zip(held, sizes, orders):
        @pl.when((own >= start) & (own < start + size))
        def _(ref=ref, start=start, order=order):
            copies = collect(ref, own - start, scratch_ref, tile_pos, order, sems)
            for copy in copies:
                copy.start()
            for copy in copies:
                copy.wait()
        start += size
    both_solves(
        split(scratch_ref[...]), solved_ref.shape[1], info_ref[1], inverse, solved_ref, scratch_ref, high_ref, low_ref
    )


def change_kernel(orders, steps, sizes, info_ref, *refs):
    refs = list(refs)
    held = [refs.pop(0) for _ in sizes]
    factor = [refs.pop(0) for _ in range(steps)]
    below, side = refs[:3], refs[3:6]
    front_below_ref, front_diag_ref, below_ref, diag_ref, token_ref, match_ref, sems = refs[6:]
    token_ref[0, 0] = 0.0
    tile_pos, col_pos = info_ref[0], info_ref[1]
    rows, width = below_ref.shape

    @pl.when(col_pos < PANELS)
    def _():
        below_ref[...] = below[0][...]

    @pl.when(col_pos >= PANELS)
    def _():
        start = 0
        for ref, size, order in zip(held, sizes, orders):
            for n in range(size):
                @pl.when((start + n + steps) // 2 == col_pos)
                def _(ref=ref, n=n, at=start + n, order=order):
                    half = match_ref.at[pl.ds((at % 2) * rows, rows), :]
                    copies = collect(ref, n, half, tile_pos, order, sems)
                    for copy in copies:
                        copy.start()
                    for copy in copies:
                        copy.wait()
            start += size
        for part in range(width // rows):
            here = slice(part * rows, (part + 1) * rows)
            match = split(match_ref[here, :])
            pair = below[1][...], below[2][...]
            below_ref[:, here] = front_below_ref[:, here] - dot3(pair, match, NT)

            @pl.when(tile_pos // 2 >= col_pos)
            def _():
                pair = side[1][...], side[2][...]
                diag_ref[:, here] = front_diag_ref[:, here] - dot3(pair, match, NT)

    @pl.when((col_pos < PANELS) & (tile_pos >= steps))
    def _():
        diag_ref[...] = side[0][...]

    for i in range(steps):
        size = (i + 1) * rows
        for panel in range(PANELS):
            @pl.when((tile_pos == i) & (col_pos == panel))
            def _(i=i, panel=panel, size=size):
                for part in range(width // rows):
                    at = panel * width + part * rows
                    here = slice(part * rows, (part + 1) * rows)
                    if at < size:
                        diag_ref[:, here] = factor[i][:, at : at + rows]

    row = lax.broadcasted_iota(jnp.int32, (rows, width), 0) + tile_pos * rows
    col = lax.broadcasted_iota(jnp.int32, (rows, width), 1) + col_pos * width
    diag_ref[...] = jnp.where(row >= col, diag_ref[...], 0.0)


def update_kernel(info_ref, row_ref, col_ref, high_ref, low_ref, *refs):
    held = [(refs[2 * k], refs[2 * k + 1]) for k in range(CHUNKS)]
    ancestor_ref, out_ref, acc_ref = refs[2 * CHUNKS :]
    rows, width = out_ref.shape
    chunk = width // CHUNKS
    even = info_ref[0] % 2 == 0
    for k, (block, other) in enumerate(held):
        for part in range(2):
            pick = even if part == 0 else jnp.logical_not(even)
            here = slice(part * rows, (part + 1) * rows)
            target = split(jnp.where(pick, block[...], other[...]))
            total = None
            for panel in range(PANELS):
                start = panel * width + k * chunk
                term = dot3(
                    (high_ref[:, start : start + chunk], low_ref[:, start : start + chunk]),
                    columns_of(target, panel * chunk, (panel + 1) * chunk),
                    NT,
                )
                total = term if total is None else total + term
            acc_ref[:, here] = total if k == 0 else acc_ref[:, here] + total
    place = lax.broadcasted_iota(jnp.int32, (rows, rows), 0)

    def move(pair, where, left):
        def one(value):
            sides = (where, value) if left else (value, where)
            dims = NN if left else NT
            return lax.dot_general(*sides, (dims, ((), ())), preferred_element_type=jnp.float32)

        return one(pair[0]) + one(pair[1])

    row_move = (row_ref[...] == place).astype(jnp.float32).astype(jnp.bfloat16)
    acc_ref[...] = move(split(acc_ref[...]), row_move, True)
    for part in range(2):
        here = slice(part * rows, (part + 1) * rows)
        col_move = (col_ref[part : part + 1, :] == place).astype(jnp.float32).astype(jnp.bfloat16)
        out_ref[:, here] = ancestor_ref[:, here] - move(split(acc_ref[:, here]), col_move, False)


def exchange(block, bit, tile_count):
    return lax.ppermute(block, "tiles", [(i, i ^ bit) for i in range(tile_count)])


def tile_bits(tile_count):
    bits, bit = [], 2
    while bit < tile_count:
        bits.append(bit)
        bit *= 2
    return bits + [1]


def climb(block, col_pos, col_count, tie, keep=None):
    held = block
    reach = 2
    while reach < col_count:
        pairs = [(at, at + reach) for at in range(reach) if at + reach < col_count]
        held = tie(held)
        other = lax.ppermute(held, "cols", pairs)
        yield [other]
        held = jnp.where(col_pos >= reach, other, held)
        reach *= 2
    held = tie(held)
    other = lax.ppermute(held, "cols", [(at, at ^ 1) for at in range(col_count)])
    if keep is not None:
        keep.extend((held, other))
    yield [other]
    return held, other


def by_panel(pair, col_pos):
    even = col_pos % 2 == 0
    return jnp.where(even, pair[0], pair[1]), jnp.where(even, pair[1], pair[0])


def gather_rows(piece, order, tile_pos, tile_count, tie):
    held = piece[None]
    for bit in order:
        held = tie(held)
        other = exchange(held, bit, tile_count)
        yield [other]
        held = jnp.concatenate((held, other), 0)
    if piece.shape[1] % 8 == 0:
        return held
    place = {}
    for m in range(tile_count):
        place[sum(bit for p, bit in enumerate(order) if m >> p & 1)] = m
    table = jnp.array([place[w] for w in range(tile_count)], jnp.int32)
    return jnp.concatenate(
        [
            lax.dynamic_index_in_dim(held, table[i ^ tile_pos], 0, keepdims=False)
            for i in range(tile_count)
        ],
        1,
    )[None]


def fetch_target(block, order, tile_pos, tile_count, target, tie):
    for bit in order[:-1]:
        block = tie(block)
        other = exchange(block, bit, tile_count)
        yield [other]
        mine = (tile_pos & bit) == ((2 * target) & bit)
        block = jnp.where(mine, block, other)
    block = tie(block)
    other = exchange(block, 1, tile_count)
    yield [other]
    return block, other


class Plan:
    def __init__(self):
        self.streams = []
        self.results = {}
        self.token = None

    def tie(self, value):
        return value if self.token is None else value + self.token[0, 0]

    def add(self, name, stream, windows):
        self.streams.append([name, stream, list(windows)])

    def run(self, window):
        flying = []
        for entry in self.streams:
            name, stream, windows = entry
            while windows and windows[0] <= window:
                windows.pop(0)
                try:
                    flying += next(stream)
                except StopIteration as stop:
                    self.results[name] = stop.value
                    windows.clear()
        return flying

    def advance(self, name, kept, key):
        for entry in self.streams:
            if entry[0] == name:
                while not kept.get(key):
                    next(entry[1])

    def finish(self, name):
        for entry in self.streams:
            if entry[0] == name:
                while name not in self.results:
                    try:
                        next(entry[1])
                    except StopIteration as stop:
                        self.results[name] = stop.value
                entry[2] = []
        return self.results[name]


CHUNKS = 4
PARTS = 2
LEAD_WINDOWS = ([1, 2, 3, 4, 5], [2, 3, 5, 6, 7], [4, 5, 6, 7, 9], [5, 6, 7, 8, 10])
SIDE_WINDOWS = ([6, 7, 8, 9, 11], [7, 8, 10, 11, 13])
BELOW_WINDOWS = ([8, 9, 10, 11, 12], [9, 10, 11, 12, 14], [10, 11, 12, 13, 15], [11, 12, 14, 15, 16])


def shards(tile_count, col_count, front_diag, front_below, ancestor, owner_cols, rel):
    rows, width = front_diag.shape
    lead = PANELS * width
    steps = lead // rows
    tile_pos = lax.axis_index("tiles")
    col_pos = lax.axis_index("cols")
    target = lax.dynamic_slice_in_dim(owner_cols, col_pos, 1)[0]
    info = jnp.stack((tile_pos, col_pos)).astype(jnp.int32)
    bits = tile_bits(tile_count)
    turned = bits[-2::-1] + [1]
    plan = Plan()
    chunk = width // CHUNKS
    own_parts = {}

    def below_stream(k, order):
        block = front_below[:, k * chunk : (k + 1) * chunk]
        own_parts[k] = []
        pair = yield from climb(block, col_pos, col_count, plan.tie, own_parts[k])
        both = jnp.concatenate(by_panel(pair, col_pos), 1)
        return (yield from fetch_target(both, order, tile_pos, tile_count, target, plan.tie))

    for k, windows in enumerate(BELOW_WINDOWS):
        plan.add(("below", k), below_stream(k, turned if k % 2 else bits), windows)
    plan.run(0)
    pieces = lax.all_to_all(
        front_diag.reshape(tile_count, rows // tile_count, width), "tiles", 0, 0, tiled=True
    )

    def lead_stream(i):
        size = (i + 1) * rows
        take = pieces[i : i + 1, :, : min(size, width)]
        pair = yield from climb(take, col_pos, col_count, plan.tie)
        panels = by_panel(pair, col_pos)
        piece = panels[0] if size <= width else jnp.concatenate(panels, 2)[:, :, :size]
        return (yield from gather_rows(piece, bits, tile_pos, tile_count, plan.tie))

    def side_stream(start, stop, order):
        pair = yield from climb(pieces[start:stop], col_pos, col_count, plan.tie)
        piece = jnp.concatenate(by_panel(pair, col_pos), 2)
        return (yield from gather_rows(piece, order, tile_pos, tile_count, plan.tie))

    for i, windows in enumerate(LEAD_WINDOWS):
        plan.add(("lead", i), lead_stream(i), windows)
    middle = steps + (tile_count - steps) // 2
    plan.add(("side", 0), side_stream(steps, middle, bits), SIDE_WINDOWS[0])
    plan.add(("side", 1), side_stream(middle, tile_count, turned), SIDE_WINDOWS[1])
    flying = []
    for window in range(1, 4):
        flying += plan.run(window)
    started = plan.run(4)

    factor_rows, inverse_rows = [], []
    window = 5
    blocks = rows // BLOCK
    cuts = sorted({blocks * p // PARTS for p in range(PARTS + 1)})
    for i in range(steps):
        held = plan.finish(("lead", i))
        state = None
        for first, last in zip(cuts[:-1], cuts[1:]):
            begun = plan.run(window)
            state = tile_part(
                i, first, last, rows, bits, info, held, state and state[:3], inverse_rows, flying
            )
            flying, started = started + begun, []
            plan.token = state[5]
            window += 1
        window = 5 + PARTS * (i + 1)
        factor_rows.append(state[0])
        inverse_rows.append(tuple(state[3:5]))
    for k in range(CHUNKS):
        plan.advance(("below", k), own_parts, k)
    begun = plan.run(window)
    pairs = [part for pair in inverse_rows for part in pair]
    solves = [
        jax.ShapeDtypeStruct((rows, width), jnp.float32),
        jax.ShapeDtypeStruct((rows, lead), jnp.bfloat16),
        jax.ShapeDtypeStruct((rows, lead), jnp.bfloat16),
        TOKEN,
    ]
    wide = pltpu.VMEM((rows, lead), jnp.float32)
    below = pl.pallas_call(
        functools.partial(below_kernel, steps),
        out_shape=solves,
        in_specs=[SMEM] + [VMEM] * (2 * CHUNKS + len(pairs)),
        out_specs=[VMEM] * 3 + [SMEM],
        scratch_shapes=[wide],
        compiler_params=limit(),
        cost_estimate=cost(20_000_000_000),
    )(info, *[part for k in range(CHUNKS) for part in own_parts[k]], *pairs)
    plan.token = below[3]
    plan.run(window + 1)
    sides = [plan.finish(("side", n)) for n in range(2)]
    sems = pltpu.SemaphoreType.DMA((sides[0].shape[0],))
    sizes = (middle - steps, tile_count - middle)
    orders = (bits, turned)
    side = pl.pallas_call(
        functools.partial(side_kernel, orders, steps, sizes),
        out_shape=solves,
        in_specs=[SMEM, ANY, ANY] + [VMEM] * len(pairs),
        out_specs=[VMEM] * 3 + [SMEM],
        scratch_shapes=[wide, sems],
        compiler_params=limit(),
        cost_estimate=cost(20_000_000_000),
    )(info, *sides, *pairs)
    plan.token = side[3]
    plan.run(window + 2)
    flat = jax.ShapeDtypeStruct((rows, width), jnp.float32)
    factor_below, factor_diag, token = pl.pallas_call(
        functools.partial(change_kernel, orders, steps, sizes),
        out_shape=[flat, flat, TOKEN],
        in_specs=[SMEM, ANY, ANY] + [VMEM] * (steps + 8),
        out_specs=[VMEM] * 2 + [SMEM],
        scratch_shapes=[pltpu.VMEM((width, lead), jnp.float32), sems],
        compiler_params=limit(),
        cost_estimate=cost(20_000_000_000),
    )(info, *sides, *factor_rows, *below[:3], *side[:3], front_below, front_diag)
    plan.token = token
    plan.run(window + 3)
    target_parts = [part for k in range(CHUNKS) for part in plan.finish(("below", k))]
    row_places = lax.dynamic_slice_in_dim(rel, tile_pos * rows, rows) - tile_pos * rows
    col_places = lax.dynamic_slice_in_dim(rel, target * width, width).reshape(2, rows)
    col_places = col_places - target * width - jnp.array([[0], [rows]], jnp.int32)
    ancestor_out = pl.pallas_call(
        update_kernel,
        out_shape=flat,
        in_specs=[SMEM] + [VMEM] * (5 + 2 * CHUNKS),
        out_specs=VMEM,
        scratch_shapes=[pltpu.VMEM((rows, width), jnp.float32)],
        compiler_params=limit(),
        cost_estimate=cost(10_000_000_000),
    )(info, row_places[None], col_places, below[1], below[2], *target_parts, ancestor)
    return (factor_diag, factor_below, ancestor_out)


def solution(mesh):
    placed = (P("tiles", "cols"), P("tiles", "cols"), P("tiles", "cols"), P(), P())
    return jax.shard_map(
        functools.partial(shards, mesh.shape["tiles"], mesh.shape["cols"]),
        mesh=mesh,
        in_specs=placed,
        out_specs=(P("tiles", "cols"), P("tiles", "cols"), P("tiles", "cols")),
        check_vma=False,
    )
```

```python
import functools

import jax
import jax.numpy as jnp
from jax import lax
from jax.experimental import pallas as pl
from jax.experimental.pallas import tpu as pltpu
from jax.sharding import PartitionSpec as P

PANELS = 2
BLOCK = 128
GROUP = 8


def factor_block(block):
    group_count = BLOCK // GROUP
    lane = lax.broadcasted_iota(jnp.int32, (GROUP, BLOCK), 1)
    sub = lax.broadcasted_iota(jnp.int32, (GROUP, BLOCK), 0)
    rows = [block[GROUP * m : GROUP * (m + 1), :] for m in range(group_count)]
    factor = [jnp.zeros((GROUP, BLOCK), jnp.float32) for _ in range(group_count)]
    inverse = []
    for s in range(group_count):
        first = GROUP * s
        columns = {
            m: [
                jnp.broadcast_to(rows[m][:, first + j : first + j + 1], (GROUP, BLOCK))
                for j in range(GROUP)
            ]
            for m in range(s, group_count)
        }
        entry = {
            (k, j): jnp.broadcast_to(columns[s][j][k : k + 1, :], (GROUP, BLOCK))
            for j in range(GROUP)
            for k in range(j, GROUP)
        }
        here = (lane >= first) & (lane < first + GROUP)
        own = jnp.where(here, (lane - first == sub).astype(jnp.float32), rows[s])
        spread = [jnp.broadcast_to(own[k : k + 1, :], (GROUP, BLOCK)) for k in range(GROUP)]
        reciprocal, ratio = [], {}
        for j in range(GROUP):
            reciprocal.append(1.0 / entry[j, j])
            for k in range(j + 1, GROUP):
                ratio[k, j] = entry[k, j] * reciprocal[j]
            for k in range(j + 1, GROUP):
                for i in range(k, GROUP):
                    entry[i, k] = entry[i, k] - entry[i, j] * ratio[k, j]
                spread[k] = spread[k] - ratio[k, j] * spread[j]
        scale = [lax.rsqrt(entry[j, j]) for j in range(GROUP)]
        for m in range(s, group_count):
            piece = columns[m]
            for k in range(GROUP):
                for j in range(k):
                    piece[k] = piece[k] - ratio[k, j] * piece[j]
                factor[m] = jnp.where(lane == first + k, piece[k] * scale[k], factor[m])
            if m > s:
                parts = [piece[k] * reciprocal[k] * spread[k] for k in range(GROUP)]
                while len(parts) > 1:
                    parts = [parts[i] + parts[i + 1] for i in range(0, len(parts), 2)]
                rows[m] = jnp.where(here, 0.0, rows[m]) - parts[0]
        done = jnp.zeros((GROUP, BLOCK), jnp.float32)
        for k in range(GROUP):
            done = jnp.where(sub == k, spread[k] * scale[k], done)
        inverse.append(jnp.where(lane <= first + sub, done, 0.0))
        factor[s] = jnp.where(lane <= first + sub, factor[s], 0.0)
    return jnp.concatenate(factor, 0), jnp.concatenate(inverse, 0)


def exact_dot(left, right, dims):
    return lax.dot_general(
        left, right, (dims, ((), ())),
        precision=lax.Precision.HIGHEST, preferred_element_type=jnp.float32,
    )


def split(value):
    high = value.astype(jnp.bfloat16)
    return high, (value - high.astype(jnp.float32)).astype(jnp.bfloat16)


NT = ((1,), (1,))
NN = ((1,), (0,))


def dot3(left, right, dims):
    def one(a, b):
        return lax.dot_general(a, b, (dims, ((), ())), preferred_element_type=jnp.float32)

    return one(left[0], right[0]) + (one(left[0], right[1]) + one(left[1], right[0]))


def columns_of(pair, start, stop):
    return pair[0][:, start:stop], pair[1][:, start:stop]


def collect(held_refs, chosen, out_ref, tile_pos, order, sems):
    def run(sources):
        copies = [
            pltpu.make_async_copy(
                ref.at[place, chosen], out_ref.at[pl.ds(i * rows, rows), :], sems.at[i]
            )
            for i, (ref, place) in enumerate(sources)
        ]
        for copy in copies:
            copy.start()
        for copy in copies:
            copy.wait()

    count, rows = held_refs[0].shape[0], held_refs[0].shape[2]
    if len(held_refs) == 1:
        run([(held_refs[0], i) for i in range(count)])
        return
    for parity in range(2):

        @pl.when(tile_pos % 2 == parity)
        def _(parity=parity):
            sources = []
            for i in range(2 * count):
                place = 0
                for p, bit in enumerate(order[:-1]):
                    place = place + (((i ^ tile_pos) // bit) % 2) * 2**p
                sources.append((held_refs[(i ^ parity) % 2], place))
            run(sources)


def tile_kernel(index, first, last, order, sources, waits, *refs):
    refs = list(refs)
    begin = first == 0
    if begin:
        info_ref = refs.pop(0)
        held_refs = [refs.pop(0) for _ in range(sources)]
    else:
        state = [refs.pop(0) for _ in range(3)]
    done_refs = [(refs.pop(0), refs.pop(0)) for _ in range(index)]
    del refs[:waits]
    l_ref, w_ref, s_ref, high_ref, low_ref, token_ref = refs[:6]
    token_ref[0, 0] = 0.0
    rows = s_ref.shape[0]
    count = rows // BLOCK
    lead = index * rows
    row = lax.broadcasted_iota(jnp.int32, (BLOCK, BLOCK), 0)
    col = lax.broadcasted_iota(jnp.int32, (BLOCK, BLOCK), 1)
    if begin:
        t_ref, sems = refs[6:]
        collect(held_refs, 0, t_ref, info_ref[0], order, sems)
        l_ref[:, lead:] = jnp.zeros((rows, rows), jnp.float32)
        w_ref[...] = jnp.zeros_like(w_ref)
        diag = t_ref[:, lead:]
        if index:
            given = split(t_ref[:, :lead])
            for j in range(index):
                end = (j + 1) * rows
                pair = done_refs[j][0][...], done_refs[j][1][...]
                l_ref[:, j * rows : end] = dot3(columns_of(given, 0, end), pair, NT)
            solved = split(l_ref[:, :lead])
            diag = diag - dot3(solved, solved, NT)
        for i in range(count):
            for j in range(i + 1):
                tile = diag[i * BLOCK : (i + 1) * BLOCK, j * BLOCK : (j + 1) * BLOCK]
                flipped = tile.T
                if i == j:
                    tile = jnp.where(row >= col, tile, flipped)
                else:
                    s_ref[j * BLOCK : (j + 1) * BLOCK, i * BLOCK : (i + 1) * BLOCK] = flipped
                s_ref[i * BLOCK : (i + 1) * BLOCK, j * BLOCK : (j + 1) * BLOCK] = tile
    else:
        for source, target in zip(state, (l_ref, w_ref, s_ref)):
            target[...] = source[...]
    lane = lax.broadcasted_iota(jnp.int32, (BLOCK, rows), 1)

    def step(b, carry):
        start = pl.multiple_of(b * BLOCK, BLOCK)
        own = pl.ds(start, BLOCK)
        own_l = pl.ds(pl.multiple_of(lead + b * BLOCK, BLOCK), BLOCK)
        lower, inverse = factor_block(s_ref[own, own])
        l_ref[own, own_l] = lower
        s_ref[own, own] = (row == col).astype(jnp.float32)
        strip = exact_dot(inverse, s_ref[own, :], NN)
        w_ref[own, :] = jnp.where(lane < start + BLOCK, strip, 0.0)

        def below(m, carry):
            these = pl.ds(pl.multiple_of(m * BLOCK, BLOCK), BLOCK)
            solved = exact_dot(s_ref[these, own], inverse, NT)
            l_ref[these, own_l] = solved
            s_ref[these, own] = jnp.zeros((BLOCK, BLOCK), jnp.float32)
            s_ref[these, :] = s_ref[these, :] - exact_dot(solved, strip, NN)
            return carry

        return lax.fori_loop(b + 1, count, below, carry)

    lax.fori_loop(first, last, step, 0)
    if last == count:
        inverse = split(w_ref[...])
        high_ref[:, lead:], low_ref[:, lead:] = inverse
        if index:
            solved = split(l_ref[:, :lead])
            for k in range(index):
                total = None
                for j in range(k, index):
                    pair = columns_of(done_refs[j], k * rows, (k + 1) * rows)
                    term = dot3(columns_of(solved, j * rows, (j + 1) * rows), pair, NN)
                    total = term if total is None else total + term
                cross = split(-dot3(inverse, split(total), NN))
                here = slice(k * rows, (k + 1) * rows)
                high_ref[:, here], low_ref[:, here] = cross


VMEM = pl.BlockSpec(memory_space=pltpu.VMEM)
SMEM = pl.BlockSpec(memory_space=pltpu.SMEM)
ANY = pl.BlockSpec(memory_space=pl.ANY)


def limit(size=60):
    return pltpu.CompilerParams(vmem_limit_bytes=size * 2**20)


def cost(flops):
    return pl.CostEstimate(flops=flops, transcendentals=0, bytes_accessed=2**20)


TOKEN = jax.ShapeDtypeStruct((1, 1), jnp.float32)


def tile_part(index, first, last, rows, order, info, held, state, done, waits):
    flat = jax.ShapeDtypeStruct((rows, rows), jnp.float32)
    wide = jax.ShapeDtypeStruct((rows, (index + 1) * rows), jnp.float32)
    half = jax.ShapeDtypeStruct((rows, (index + 1) * rows), jnp.bfloat16)
    begin = first == 0
    given = [info, *held] if begin else list(state)
    pairs = [part for pair in done for part in pair]
    return pl.pallas_call(
        functools.partial(tile_kernel, index, first, last, order, len(held), len(waits)),
        out_shape=[wide, flat, flat, half, half, TOKEN],
        in_specs=([SMEM] + [ANY] * len(held) if begin else [VMEM] * 3) + [VMEM] * len(pairs) + [ANY] * len(waits),
        out_specs=[VMEM] * 5 + [SMEM],
        scratch_shapes=[
            pltpu.VMEM((rows, (index + 1) * rows), jnp.float32),
            pltpu.SemaphoreType.DMA((held[0].shape[0] * len(held),)),
        ] if begin else [],
        compiler_params=limit(),
        cost_estimate=cost((last - first) * 8_000_000_000),
    )(*given, *pairs, *waits)


def both_solves(source, width, panel, inverse, solved_ref, scratch_ref, high_ref, low_ref):
    rows = source[0].shape[0]
    steps = len(inverse)
    step = inverse[0][0].shape[0]
    for j in range(steps):
        pair = inverse[j][0][...], inverse[j][1][...]
        scratch_ref[:, j * step : (j + 1) * step] = dot3(
            columns_of(source, 0, (j + 1) * step), pair, NT
        )
    solved_ref[...] = jnp.where(panel == 0, scratch_ref[:, :width], scratch_ref[:, width:])
    solved = split(scratch_ref[...])
    for k in range(steps):
        total = None
        for j in range(k, steps):
            pair = columns_of(inverse[j], k * step, (k + 1) * step)
            term = dot3(columns_of(solved, j * step, (j + 1) * step), pair, NN)
            total = term if total is None else total + term
        here = slice(k * step, (k + 1) * step)
        high_ref[:, here], low_ref[:, here] = split(total)


def below_kernel(steps, info_ref, *refs):
    refs = list(refs)
    held = [(refs.pop(0), refs.pop(0)) for _ in range(CHUNKS)]
    inverse = [(refs.pop(0), refs.pop(0)) for _ in range(steps)]
    solved_ref, high_ref, low_ref, token_ref, scratch_ref = refs
    token_ref[0, 0] = 0.0
    width = solved_ref.shape[1]
    chunk = width // CHUNKS
    even = info_ref[1] % 2 == 0
    for k, (own, other) in enumerate(held):
        for panel in range(PANELS):
            start = panel * width + k * chunk
            pick = even if panel == 0 else jnp.logical_not(even)
            scratch_ref[:, start : start + chunk] = jnp.where(pick, own[...], other[...])
    both_solves(
        split(scratch_ref[...]), width, info_ref[1], inverse, solved_ref, scratch_ref, high_ref, low_ref
    )


def side_kernel(steps, info_ref, held_ref, *refs):
    refs = list(refs)
    inverse = [(refs.pop(0), refs.pop(0)) for _ in range(steps)]
    solved_ref, high_ref, low_ref, token_ref, scratch_ref, sems = refs
    token_ref[0, 0] = 0.0
    own = jnp.maximum(info_ref[0] - steps, 0)
    collect([held_ref], own, scratch_ref, info_ref[0], None, sems)
    both_solves(
        split(scratch_ref[...]), solved_ref.shape[1], info_ref[1], inverse, solved_ref, scratch_ref, high_ref, low_ref
    )


def change_kernel(steps, info_ref, held_ref, *refs):
    refs = list(refs)
    factor = [refs.pop(0) for _ in range(steps)]
    below, side = refs[:3], refs[3:6]
    front_below_ref, front_diag_ref, below_ref, diag_ref, token_ref, match_ref, sems = refs[6:]
    token_ref[0, 0] = 0.0
    tile_pos, col_pos = info_ref[0], info_ref[1]
    rows, width = below_ref.shape

    @pl.when(col_pos < PANELS)
    def _():
        below_ref[...] = below[0][...]

    @pl.when(col_pos >= PANELS)
    def _():
        for half in range(2):
            part = match_ref.at[pl.ds(half * rows, rows), :]
            collect([held_ref], 2 * col_pos + half - steps, part, tile_pos, None, sems)
        for part in range(width // rows):
            here = slice(part * rows, (part + 1) * rows)
            match = split(match_ref[here, :])
            pair = below[1][...], below[2][...]
            below_ref[:, here] = front_below_ref[:, here] - dot3(pair, match, NT)

            @pl.when(tile_pos // 2 >= col_pos)
            def _():
                pair = side[1][...], side[2][...]
                diag_ref[:, here] = front_diag_ref[:, here] - dot3(pair, match, NT)

    @pl.when((col_pos < PANELS) & (tile_pos >= steps))
    def _():
        diag_ref[...] = side[0][...]

    for i in range(steps):
        size = (i + 1) * rows
        for panel in range(PANELS):
            @pl.when((tile_pos == i) & (col_pos == panel))
            def _(i=i, panel=panel, size=size):
                for part in range(width // rows):
                    at = panel * width + part * rows
                    here = slice(part * rows, (part + 1) * rows)
                    if at < size:
                        diag_ref[:, here] = factor[i][:, at : at + rows]

    row = lax.broadcasted_iota(jnp.int32, (rows, width), 0) + tile_pos * rows
    col = lax.broadcasted_iota(jnp.int32, (rows, width), 1) + col_pos * width
    diag_ref[...] = jnp.where(row >= col, diag_ref[...], 0.0)


def update_kernel(info_ref, row_ref, col_ref, high_ref, low_ref, *refs):
    held = [(refs[2 * k], refs[2 * k + 1]) for k in range(CHUNKS)]
    ancestor_ref, out_ref, acc_ref = refs[2 * CHUNKS :]
    rows, width = out_ref.shape
    chunk = width // CHUNKS
    even = info_ref[0] % 2 == 0
    for k, (block, other) in enumerate(held):
        for part in range(2):
            pick = even if part == 0 else jnp.logical_not(even)
            here = slice(part * rows, (part + 1) * rows)
            target = split(jnp.where(pick, block[...], other[...]))
            total = None
            for panel in range(PANELS):
                start = panel * width + k * chunk
                term = dot3(
                    (high_ref[:, start : start + chunk], low_ref[:, start : start + chunk]),
                    columns_of(target, panel * chunk, (panel + 1) * chunk),
                    NT,
                )
                total = term if total is None else total + term
            acc_ref[:, here] = total if k == 0 else acc_ref[:, here] + total
    place = lax.broadcasted_iota(jnp.int32, (rows, rows), 0)

    def move(pair, where, left):
        def one(value):
            sides = (where, value) if left else (value, where)
            dims = NN if left else NT
            return lax.dot_general(*sides, (dims, ((), ())), preferred_element_type=jnp.float32)

        return one(pair[0]) + one(pair[1])

    row_move = (row_ref[...] == place).astype(jnp.float32).astype(jnp.bfloat16)
    acc_ref[...] = move(split(acc_ref[...]), row_move, True)
    for part in range(2):
        here = slice(part * rows, (part + 1) * rows)
        col_move = (col_ref[part : part + 1, :] == place).astype(jnp.float32).astype(jnp.bfloat16)
        out_ref[:, here] = ancestor_ref[:, here] - move(split(acc_ref[:, here]), col_move, False)


def exchange(block, bit, tile_count):
    return lax.ppermute(block, "tiles", [(i, i ^ bit) for i in range(tile_count)])


def tile_bits(tile_count):
    bits, bit = [], 2
    while bit < tile_count:
        bits.append(bit)
        bit *= 2
    return bits + [1]


def climb(block, col_pos, col_count, tie, keep=None):
    held = block
    reach = 2
    while reach < col_count:
        pairs = [(at, at + reach) for at in range(reach) if at + reach < col_count]
        held = tie(held)
        other = lax.ppermute(held, "cols", pairs)
        yield [other]
        held = jnp.where(col_pos >= reach, other, held)
        reach *= 2
    held = tie(held)
    other = lax.ppermute(held, "cols", [(at, at ^ 1) for at in range(col_count)])
    if keep is not None:
        keep.extend((held, other))
    yield [other]
    return held, other


def by_panel(pair, col_pos):
    even = col_pos % 2 == 0
    return jnp.where(even, pair[0], pair[1]), jnp.where(even, pair[1], pair[0])


def gather_rows(piece, order, tile_pos, tile_count, tie):
    held = piece[None]
    for bit in order:
        held = tie(held)
        other = exchange(held, bit, tile_count)
        yield [other]
        if bit == 1 and piece.shape[1] % 8 == 0:
            return held, other
        held = jnp.concatenate((held, other), 0)
    place = {}
    for m in range(tile_count):
        place[sum(bit for p, bit in enumerate(order) if m >> p & 1)] = m
    table = jnp.array([place[w] for w in range(tile_count)], jnp.int32)
    ordered = jnp.concatenate(
        [
            lax.dynamic_index_in_dim(held, table[i ^ tile_pos], 0, keepdims=False)
            for i in range(tile_count)
        ],
        1,
    )
    return (ordered[None],)


def fetch_target(block, order, tile_pos, tile_count, target, tie):
    for bit in order[:-1]:
        block = tie(block)
        other = exchange(block, bit, tile_count)
        yield [other]
        mine = (tile_pos & bit) == ((2 * target) & bit)
        block = jnp.where(mine, block, other)
    block = tie(block)
    other = exchange(block, 1, tile_count)
    yield [other]
    return block, other


class Plan:
    def __init__(self):
        self.streams = []
        self.results = {}
        self.token = None

    def tie(self, value):
        return value if self.token is None else value + self.token[0, 0]

    def add(self, name, stream, windows):
        self.streams.append([name, stream, list(windows)])

    def run(self, window):
        flying = []
        for entry in self.streams:
            name, stream, windows = entry
            while windows and windows[0] <= window:
                windows.pop(0)
                try:
                    flying += next(stream)
                except StopIteration as stop:
                    self.results[name] = stop.value
                    windows.clear()
        return flying

    def advance(self, name, kept, key):
        for entry in self.streams:
            if entry[0] == name:
                while not kept.get(key):
                    next(entry[1])

    def finish(self, name):
        for entry in self.streams:
            if entry[0] == name:
                while name not in self.results:
                    try:
                        next(entry[1])
                    except StopIteration as stop:
                        self.results[name] = stop.value
                entry[2] = []
        return self.results[name]


CHUNKS = 2
PARTS = 2
LEAD_WINDOWS = ([1, 2, 3, 4, 5], [2, 3, 5, 6, 7], [4, 5, 6, 7, 9], [5, 6, 7, 8, 10])
SIDE_WINDOWS = [6, 7, 8]
BELOW_WINDOWS = ([7, 8, 9, 10, 11], [8, 9, 11, 12, 13])


def shards(tile_count, col_count, front_diag, front_below, ancestor, owner_cols, rel):
    rows, width = front_diag.shape
    lead = PANELS * width
    steps = lead // rows
    tile_pos = lax.axis_index("tiles")
    col_pos = lax.axis_index("cols")
    target = lax.dynamic_slice_in_dim(owner_cols, col_pos, 1)[0]
    info = jnp.stack((tile_pos, col_pos)).astype(jnp.int32)
    bits = tile_bits(tile_count)
    turned = bits[-2::-1] + [1]
    plan = Plan()
    chunk = width // CHUNKS
    own_parts = {}

    def below_stream(k, order):
        block = front_below[:, k * chunk : (k + 1) * chunk]
        own_parts[k] = []
        pair = yield from climb(block, col_pos, col_count, plan.tie, own_parts[k])
        both = jnp.concatenate(by_panel(pair, col_pos), 1)
        return (yield from fetch_target(both, order, tile_pos, tile_count, target, plan.tie))

    for k, windows in enumerate(BELOW_WINDOWS):
        plan.add(("below", k), below_stream(k, turned if k % 2 else bits), windows)
    plan.run(0)
    pieces = lax.all_to_all(
        front_diag.reshape(tile_count, rows // tile_count, width), "tiles", 0, 0, tiled=True
    )

    def lead_stream(i):
        size = (i + 1) * rows
        take = pieces[i : i + 1, :, : min(size, width)]
        pair = yield from climb(take, col_pos, col_count, plan.tie)
        panels = by_panel(pair, col_pos)
        piece = panels[0] if size <= width else jnp.concatenate(panels, 2)[:, :, :size]
        return (yield from gather_rows(piece, bits, tile_pos, tile_count, plan.tie))

    def side_stream():
        pair = yield from climb(pieces[steps:], col_pos, col_count, plan.tie)
        piece = plan.tie(jnp.concatenate(by_panel(pair, col_pos), 2))
        held = lax.all_gather(piece, "tiles")
        yield []
        if piece.shape[1] % 8:
            held = jnp.swapaxes(held, 0, 1).reshape(1, tile_count - steps, rows, lead)
        return held

    for i, windows in enumerate(LEAD_WINDOWS):
        plan.add(("lead", i), lead_stream(i), windows)
    plan.add("side", side_stream(), SIDE_WINDOWS)
    flying = []
    for window in range(1, 4):
        flying += plan.run(window)
    started = plan.run(4)

    factor_rows, inverse_rows = [], []
    window = 5
    blocks = rows // BLOCK
    cuts = sorted({blocks * p // PARTS for p in range(PARTS + 1)})
    for i in range(steps):
        held = plan.finish(("lead", i))
        state = None
        for first, last in zip(cuts[:-1], cuts[1:]):
            begun = plan.run(window)
            state = tile_part(
                i, first, last, rows, bits, info, held, state and state[:3], inverse_rows, flying
            )
            flying, started = started + begun, []
            plan.token = state[5]
            window += 1
        window = 5 + PARTS * (i + 1)
        factor_rows.append(state[0])
        inverse_rows.append(tuple(state[3:5]))
    for k in range(CHUNKS):
        plan.advance(("below", k), own_parts, k)
    begun = plan.run(window)
    pairs = [part for pair in inverse_rows for part in pair]
    solves = [
        jax.ShapeDtypeStruct((rows, width), jnp.float32),
        jax.ShapeDtypeStruct((rows, lead), jnp.bfloat16),
        jax.ShapeDtypeStruct((rows, lead), jnp.bfloat16),
        TOKEN,
    ]
    wide = pltpu.VMEM((rows, lead), jnp.float32)
    below = pl.pallas_call(
        functools.partial(below_kernel, steps),
        out_shape=solves,
        in_specs=[SMEM] + [VMEM] * (2 * CHUNKS + len(pairs)),
        out_specs=[VMEM] * 3 + [SMEM],
        scratch_shapes=[wide],
        compiler_params=limit(),
        cost_estimate=cost(20_000_000_000),
    )(info, *[part for k in range(CHUNKS) for part in own_parts[k]], *pairs)
    plan.token = below[3]
    plan.run(window + 1)
    gathered = plan.finish("side")
    sems = pltpu.SemaphoreType.DMA((gathered.shape[0],))
    side = pl.pallas_call(
        functools.partial(side_kernel, steps),
        out_shape=solves,
        in_specs=[SMEM, ANY] + [VMEM] * len(pairs),
        out_specs=[VMEM] * 3 + [SMEM],
        scratch_shapes=[wide, sems],
        compiler_params=limit(),
        cost_estimate=cost(20_000_000_000),
    )(info, gathered, *pairs)
    plan.token = side[3]
    plan.run(window + 2)
    flat = jax.ShapeDtypeStruct((rows, width), jnp.float32)
    factor_below, factor_diag, token = pl.pallas_call(
        functools.partial(change_kernel, steps),
        out_shape=[flat, flat, TOKEN],
        in_specs=[SMEM, ANY] + [VMEM] * (steps + 8),
        out_specs=[VMEM] * 2 + [SMEM],
        scratch_shapes=[pltpu.VMEM((width, lead), jnp.float32), sems],
        compiler_params=limit(),
        cost_estimate=cost(20_000_000_000),
    )(info, gathered, *factor_rows, *below[:3], *side[:3], front_below, front_diag)
    plan.token = token
    plan.run(window + 3)
    target_parts = [part for k in range(CHUNKS) for part in plan.finish(("below", k))]
    row_places = lax.dynamic_slice_in_dim(rel, tile_pos * rows, rows) - tile_pos * rows
    col_places = lax.dynamic_slice_in_dim(rel, target * width, width).reshape(2, rows)
    col_places = col_places - target * width - jnp.array([[0], [rows]], jnp.int32)
    ancestor_out = pl.pallas_call(
        update_kernel,
        out_shape=flat,
        in_specs=[SMEM] + [VMEM] * (5 + 2 * CHUNKS),
        out_specs=VMEM,
        scratch_shapes=[pltpu.VMEM((rows, width), jnp.float32)],
        compiler_params=limit(),
        cost_estimate=cost(10_000_000_000),
    )(info, row_places[None], col_places, below[1], below[2], *target_parts, ancestor)
    return (factor_diag, factor_below, ancestor_out)


def solution(mesh):
    placed = (P("tiles", "cols"), P("tiles", "cols"), P("tiles", "cols"), P(), P())
    return jax.shard_map(
        functools.partial(shards, mesh.shape["tiles"], mesh.shape["cols"]),
        mesh=mesh,
        in_specs=placed,
        out_specs=(P("tiles", "cols"), P("tiles", "cols"), P("tiles", "cols")),
        check_vma=False,
    )
```

```python
import functools

import jax
import jax.numpy as jnp
from jax import lax
from jax.experimental import pallas as pl
from jax.experimental.pallas import tpu as pltpu
from jax.sharding import PartitionSpec as P

PANELS = 2
BLOCK = 128
GROUP = 8


def factor_block(block):
    group_count = BLOCK // GROUP
    lane = lax.broadcasted_iota(jnp.int32, (GROUP, BLOCK), 1)
    sub = lax.broadcasted_iota(jnp.int32, (GROUP, BLOCK), 0)
    rows = [block[GROUP * m : GROUP * (m + 1), :] for m in range(group_count)]
    factor = [jnp.zeros((GROUP, BLOCK), jnp.float32) for _ in range(group_count)]
    inverse = []
    for s in range(group_count):
        first = GROUP * s
        columns = {
            m: [
                jnp.broadcast_to(rows[m][:, first + j : first + j + 1], (GROUP, BLOCK))
                for j in range(GROUP)
            ]
            for m in range(s, group_count)
        }
        entry = {
            (k, j): jnp.broadcast_to(columns[s][j][k : k + 1, :], (GROUP, BLOCK))
            for j in range(GROUP)
            for k in range(j, GROUP)
        }
        here = (lane >= first) & (lane < first + GROUP)
        own = jnp.where(here, (lane - first == sub).astype(jnp.float32), rows[s])
        spread = [jnp.broadcast_to(own[k : k + 1, :], (GROUP, BLOCK)) for k in range(GROUP)]
        reciprocal, ratio = [], {}
        for j in range(GROUP):
            reciprocal.append(1.0 / entry[j, j])
            for k in range(j + 1, GROUP):
                ratio[k, j] = entry[k, j] * reciprocal[j]
            for k in range(j + 1, GROUP):
                for i in range(k, GROUP):
                    entry[i, k] = entry[i, k] - entry[i, j] * ratio[k, j]
                spread[k] = spread[k] - ratio[k, j] * spread[j]
        scale = [lax.rsqrt(entry[j, j]) for j in range(GROUP)]
        for m in range(s, group_count):
            piece = columns[m]
            for k in range(GROUP):
                for j in range(k):
                    piece[k] = piece[k] - ratio[k, j] * piece[j]
                factor[m] = jnp.where(lane == first + k, piece[k] * scale[k], factor[m])
            if m > s:
                parts = [piece[k] * reciprocal[k] * spread[k] for k in range(GROUP)]
                while len(parts) > 1:
                    parts = [parts[i] + parts[i + 1] for i in range(0, len(parts), 2)]
                rows[m] = jnp.where(here, 0.0, rows[m]) - parts[0]
        done = jnp.zeros((GROUP, BLOCK), jnp.float32)
        for k in range(GROUP):
            done = jnp.where(sub == k, spread[k] * scale[k], done)
        inverse.append(jnp.where(lane <= first + sub, done, 0.0))
        factor[s] = jnp.where(lane <= first + sub, factor[s], 0.0)
    return jnp.concatenate(factor, 0), jnp.concatenate(inverse, 0)


def exact_dot(left, right, dims):
    return lax.dot_general(
        left, right, (dims, ((), ())),
        precision=lax.Precision.HIGHEST, preferred_element_type=jnp.float32,
    )


def split(value):
    high = value.astype(jnp.bfloat16)
    return high, (value - high.astype(jnp.float32)).astype(jnp.bfloat16)


NT = ((1,), (1,))
NN = ((1,), (0,))


def dot3(left, right, dims):
    def one(a, b):
        return lax.dot_general(a, b, (dims, ((), ())), preferred_element_type=jnp.float32)

    return one(left[0], right[0]) + (one(left[0], right[1]) + one(left[1], right[0]))


def columns_of(pair, start, stop):
    return pair[0][:, start:stop], pair[1][:, start:stop]


def collect(held_refs, chosen, out_ref, tile_pos, order, sems):
    def run(sources):
        copies = [
            pltpu.make_async_copy(
                ref.at[place, chosen], out_ref.at[pl.ds(i * rows, rows), :], sems.at[i]
            )
            for i, (ref, place) in enumerate(sources)
        ]
        for copy in copies:
            copy.start()
        for copy in copies:
            copy.wait()

    count, rows = held_refs[0].shape[0], held_refs[0].shape[2]
    if len(held_refs) == 1:
        run([(held_refs[0], i) for i in range(count)])
        return
    for parity in range(2):

        @pl.when(tile_pos % 2 == parity)
        def _(parity=parity):
            sources = []
            for i in range(2 * count):
                place = 0
                for p, bit in enumerate(order[:-1]):
                    place = place + (((i ^ tile_pos) // bit) % 2) * 2**p
                sources.append((held_refs[(i ^ parity) % 2], place))
            run(sources)


def tile_kernel(index, first, last, order, sources, waits, *refs):
    refs = list(refs)
    begin = first == 0
    if begin:
        info_ref = refs.pop(0)
        held_refs = [refs.pop(0) for _ in range(sources)]
    else:
        state = [refs.pop(0) for _ in range(3)]
    done_refs = [(refs.pop(0), refs.pop(0)) for _ in range(index)]
    del refs[:waits]
    l_ref, w_ref, s_ref, high_ref, low_ref, token_ref = refs[:6]
    token_ref[0, 0] = 0.0
    rows = s_ref.shape[0]
    count = rows // BLOCK
    lead = index * rows
    row = lax.broadcasted_iota(jnp.int32, (BLOCK, BLOCK), 0)
    col = lax.broadcasted_iota(jnp.int32, (BLOCK, BLOCK), 1)
    if begin:
        t_ref, sems = refs[6:]
        collect(held_refs, 0, t_ref, info_ref[0], order, sems)
        l_ref[:, lead:] = jnp.zeros((rows, rows), jnp.float32)
        w_ref[...] = jnp.zeros_like(w_ref)
        diag = t_ref[:, lead:]
        if index:
            given = split(t_ref[:, :lead])
            for j in range(index):
                end = (j + 1) * rows
                pair = done_refs[j][0][...], done_refs[j][1][...]
                l_ref[:, j * rows : end] = dot3(columns_of(given, 0, end), pair, NT)
            solved = split(l_ref[:, :lead])
            diag = diag - dot3(solved, solved, NT)
        for i in range(count):
            for j in range(i + 1):
                tile = diag[i * BLOCK : (i + 1) * BLOCK, j * BLOCK : (j + 1) * BLOCK]
                flipped = tile.T
                if i == j:
                    tile = jnp.where(row >= col, tile, flipped)
                else:
                    s_ref[j * BLOCK : (j + 1) * BLOCK, i * BLOCK : (i + 1) * BLOCK] = flipped
                s_ref[i * BLOCK : (i + 1) * BLOCK, j * BLOCK : (j + 1) * BLOCK] = tile
    else:
        for source, target in zip(state, (l_ref, w_ref, s_ref)):
            target[...] = source[...]
    lane = lax.broadcasted_iota(jnp.int32, (BLOCK, rows), 1)

    def step(b, carry):
        start = pl.multiple_of(b * BLOCK, BLOCK)
        own = pl.ds(start, BLOCK)
        own_l = pl.ds(pl.multiple_of(lead + b * BLOCK, BLOCK), BLOCK)
        lower, inverse = factor_block(s_ref[own, own])
        l_ref[own, own_l] = lower
        s_ref[own, own] = (row == col).astype(jnp.float32)
        strip = exact_dot(inverse, s_ref[own, :], NN)
        w_ref[own, :] = jnp.where(lane < start + BLOCK, strip, 0.0)

        def below(m, carry):
            these = pl.ds(pl.multiple_of(m * BLOCK, BLOCK), BLOCK)
            solved = exact_dot(s_ref[these, own], inverse, NT)
            l_ref[these, own_l] = solved
            s_ref[these, own] = jnp.zeros((BLOCK, BLOCK), jnp.float32)
            s_ref[these, :] = s_ref[these, :] - exact_dot(solved, strip, NN)
            return carry

        return lax.fori_loop(b + 1, count, below, carry)

    lax.fori_loop(first, last, step, 0)
    if last == count:
        inverse = split(w_ref[...])
        high_ref[:, lead:], low_ref[:, lead:] = inverse
        if index:
            solved = split(l_ref[:, :lead])
            for k in range(index):
                total = None
                for j in range(k, index):
                    pair = columns_of(done_refs[j], k * rows, (k + 1) * rows)
                    term = dot3(columns_of(solved, j * rows, (j + 1) * rows), pair, NN)
                    total = term if total is None else total + term
                cross = split(-dot3(inverse, split(total), NN))
                here = slice(k * rows, (k + 1) * rows)
                high_ref[:, here], low_ref[:, here] = cross


VMEM = pl.BlockSpec(memory_space=pltpu.VMEM)
SMEM = pl.BlockSpec(memory_space=pltpu.SMEM)
ANY = pl.BlockSpec(memory_space=pl.ANY)


def limit(size=60):
    return pltpu.CompilerParams(vmem_limit_bytes=size * 2**20)


def cost(flops):
    return pl.CostEstimate(flops=flops, transcendentals=0, bytes_accessed=2**20)


TOKEN = jax.ShapeDtypeStruct((1, 1), jnp.float32)


def tile_part(index, first, last, rows, order, info, held, state, done, waits):
    flat = jax.ShapeDtypeStruct((rows, rows), jnp.float32)
    wide = jax.ShapeDtypeStruct((rows, (index + 1) * rows), jnp.float32)
    half = jax.ShapeDtypeStruct((rows, (index + 1) * rows), jnp.bfloat16)
    begin = first == 0
    given = [info, *held] if begin else list(state)
    pairs = [part for pair in done for part in pair]
    return pl.pallas_call(
        functools.partial(tile_kernel, index, first, last, order, len(held), len(waits)),
        out_shape=[wide, flat, flat, half, half, TOKEN],
        in_specs=([SMEM] + [ANY] * len(held) if begin else [VMEM] * 3) + [VMEM] * len(pairs) + [ANY] * len(waits),
        out_specs=[VMEM] * 5 + [SMEM],
        scratch_shapes=[
            pltpu.VMEM((rows, (index + 1) * rows), jnp.float32),
            pltpu.SemaphoreType.DMA((held[0].shape[0] * len(held),)),
        ] if begin else [],
        compiler_params=limit(),
        cost_estimate=cost((last - first) * 8_000_000_000),
    )(*given, *pairs, *waits)


def both_solves(source, width, panel, inverse, solved_ref, scratch_ref, high_ref, low_ref):
    rows = source[0].shape[0]
    steps = len(inverse)
    step = inverse[0][0].shape[0]
    for j in range(steps):
        pair = inverse[j][0][...], inverse[j][1][...]
        scratch_ref[:, j * step : (j + 1) * step] = dot3(
            columns_of(source, 0, (j + 1) * step), pair, NT
        )
    solved_ref[...] = jnp.where(panel == 0, scratch_ref[:, :width], scratch_ref[:, width:])
    solved = split(scratch_ref[...])
    for k in range(steps):
        total = None
        for j in range(k, steps):
            pair = columns_of(inverse[j], k * step, (k + 1) * step)
            term = dot3(columns_of(solved, j * step, (j + 1) * step), pair, NN)
            total = term if total is None else total + term
        here = slice(k * step, (k + 1) * step)
        high_ref[:, here], low_ref[:, here] = split(total)


def below_kernel(steps, info_ref, *refs):
    refs = list(refs)
    held = [(refs.pop(0), refs.pop(0)) for _ in range(CHUNKS)]
    inverse = [(refs.pop(0), refs.pop(0)) for _ in range(steps)]
    solved_ref, high_ref, low_ref, token_ref, scratch_ref = refs
    token_ref[0, 0] = 0.0
    width = solved_ref.shape[1]
    chunk = width // CHUNKS
    even = info_ref[1] % 2 == 0
    for k, (own, other) in enumerate(held):
        for panel in range(PANELS):
            start = panel * width + k * chunk
            pick = even if panel == 0 else jnp.logical_not(even)
            scratch_ref[:, start : start + chunk] = jnp.where(pick, own[...], other[...])
    both_solves(
        split(scratch_ref[...]), width, info_ref[1], inverse, solved_ref, scratch_ref, high_ref, low_ref
    )


def side_kernel(steps, info_ref, held_ref, *refs):
    refs = list(refs)
    inverse = [(refs.pop(0), refs.pop(0)) for _ in range(steps)]
    solved_ref, high_ref, low_ref, token_ref, scratch_ref, sems = refs
    token_ref[0, 0] = 0.0
    own = jnp.maximum(info_ref[0] - steps, 0)
    collect([held_ref], own, scratch_ref, info_ref[0], None, sems)
    both_solves(
        split(scratch_ref[...]), solved_ref.shape[1], info_ref[1], inverse, solved_ref, scratch_ref, high_ref, low_ref
    )


def change_kernel(steps, info_ref, held_ref, *refs):
    refs = list(refs)
    factor = [refs.pop(0) for _ in range(steps)]
    below, side = refs[:3], refs[3:6]
    front_below_ref, front_diag_ref, below_ref, diag_ref, token_ref, match_ref, sems = refs[6:]
    token_ref[0, 0] = 0.0
    tile_pos, col_pos = info_ref[0], info_ref[1]
    rows, width = below_ref.shape

    @pl.when(col_pos < PANELS)
    def _():
        below_ref[...] = below[0][...]

    @pl.when(col_pos >= PANELS)
    def _():
        for half in range(2):
            part = match_ref.at[pl.ds(half * rows, rows), :]
            collect([held_ref], 2 * col_pos + half - steps, part, tile_pos, None, sems)
        for part in range(width // rows):
            here = slice(part * rows, (part + 1) * rows)
            match = split(match_ref[here, :])
            pair = below[1][...], below[2][...]
            below_ref[:, here] = front_below_ref[:, here] - dot3(pair, match, NT)

            @pl.when(tile_pos // 2 >= col_pos)
            def _():
                pair = side[1][...], side[2][...]
                diag_ref[:, here] = front_diag_ref[:, here] - dot3(pair, match, NT)

    @pl.when((col_pos < PANELS) & (tile_pos >= steps))
    def _():
        diag_ref[...] = side[0][...]

    for i in range(steps):
        size = (i + 1) * rows
        for panel in range(PANELS):
            @pl.when((tile_pos == i) & (col_pos == panel))
            def _(i=i, panel=panel, size=size):
                for part in range(width // rows):
                    at = panel * width + part * rows
                    here = slice(part * rows, (part + 1) * rows)
                    if at < size:
                        diag_ref[:, here] = factor[i][:, at : at + rows]

    row = lax.broadcasted_iota(jnp.int32, (rows, width), 0) + tile_pos * rows
    col = lax.broadcasted_iota(jnp.int32, (rows, width), 1) + col_pos * width
    diag_ref[...] = jnp.where(row >= col, diag_ref[...], 0.0)


def update_kernel(info_ref, row_ref, col_ref, high_ref, low_ref, *refs):
    held = [(refs[2 * k], refs[2 * k + 1]) for k in range(CHUNKS)]
    ancestor_ref, out_ref, acc_ref = refs[2 * CHUNKS :]
    rows, width = out_ref.shape
    chunk = width // CHUNKS
    even = info_ref[0] % 2 == 0
    for k, (block, other) in enumerate(held):
        for part in range(2):
            pick = even if part == 0 else jnp.logical_not(even)
            here = slice(part * rows, (part + 1) * rows)
            target = split(jnp.where(pick, block[...], other[...]))
            total = None
            for panel in range(PANELS):
                start = panel * width + k * chunk
                term = dot3(
                    (high_ref[:, start : start + chunk], low_ref[:, start : start + chunk]),
                    columns_of(target, panel * chunk, (panel + 1) * chunk),
                    NT,
                )
                total = term if total is None else total + term
            acc_ref[:, here] = total if k == 0 else acc_ref[:, here] + total
    place = lax.broadcasted_iota(jnp.int32, (rows, rows), 0)

    def move(pair, where, left):
        def one(value):
            sides = (where, value) if left else (value, where)
            dims = NN if left else NT
            return lax.dot_general(*sides, (dims, ((), ())), preferred_element_type=jnp.float32)

        return one(pair[0]) + one(pair[1])

    row_move = (row_ref[...] == place).astype(jnp.float32).astype(jnp.bfloat16)
    acc_ref[...] = move(split(acc_ref[...]), row_move, True)
    for part in range(2):
        here = slice(part * rows, (part + 1) * rows)
        col_move = (col_ref[part : part + 1, :] == place).astype(jnp.float32).astype(jnp.bfloat16)
        out_ref[:, here] = ancestor_ref[:, here] - move(split(acc_ref[:, here]), col_move, False)


def exchange(block, bit, tile_count):
    return lax.ppermute(block, "tiles", [(i, i ^ bit) for i in range(tile_count)])


def tile_bits(tile_count):
    bits, bit = [], 2
    while bit < tile_count:
        bits.append(bit)
        bit *= 2
    return bits + [1]


def climb(block, col_pos, col_count, tie, keep=None):
    held = block
    reach = 2
    while reach < col_count:
        pairs = [(at, at + reach) for at in range(reach) if at + reach < col_count]
        held = tie(held)
        other = lax.ppermute(held, "cols", pairs)
        yield [other]
        held = jnp.where(col_pos >= reach, other, held)
        reach *= 2
    held = tie(held)
    other = lax.ppermute(held, "cols", [(at, at ^ 1) for at in range(col_count)])
    if keep is not None:
        keep.extend((held, other))
    yield [other]
    return held, other


def by_panel(pair, col_pos):
    even = col_pos % 2 == 0
    return jnp.where(even, pair[0], pair[1]), jnp.where(even, pair[1], pair[0])


def gather_rows(piece, order, tile_pos, tile_count, tie):
    held = piece[None]
    for bit in order:
        held = tie(held)
        other = exchange(held, bit, tile_count)
        yield [other]
        if bit == 1 and piece.shape[1] % 8 == 0:
            return held, other
        held = jnp.concatenate((held, other), 0)
    place = {}
    for m in range(tile_count):
        place[sum(bit for p, bit in enumerate(order) if m >> p & 1)] = m
    table = jnp.array([place[w] for w in range(tile_count)], jnp.int32)
    ordered = jnp.concatenate(
        [
            lax.dynamic_index_in_dim(held, table[i ^ tile_pos], 0, keepdims=False)
            for i in range(tile_count)
        ],
        1,
    )
    return (ordered[None],)


def fetch_target(block, order, tile_pos, tile_count, target, tie):
    for bit in order[:-1]:
        block = tie(block)
        other = exchange(block, bit, tile_count)
        yield [other]
        mine = (tile_pos & bit) == ((2 * target) & bit)
        block = jnp.where(mine, block, other)
    block = tie(block)
    other = exchange(block, 1, tile_count)
    yield [other]
    return block, other


class Plan:
    def __init__(self):
        self.streams = []
        self.results = {}
        self.token = None

    def tie(self, value):
        return value if self.token is None else value + self.token[0, 0]

    def add(self, name, stream, windows):
        self.streams.append([name, stream, list(windows)])

    def run(self, window):
        flying = []
        for entry in self.streams:
            name, stream, windows = entry
            while windows and windows[0] <= window:
                windows.pop(0)
                try:
                    flying += next(stream)
                except StopIteration as stop:
                    self.results[name] = stop.value
                    windows.clear()
        return flying

    def advance(self, name, kept, key):
        for entry in self.streams:
            if entry[0] == name:
                while not kept.get(key):
                    next(entry[1])

    def finish(self, name):
        for entry in self.streams:
            if entry[0] == name:
                while name not in self.results:
                    try:
                        next(entry[1])
                    except StopIteration as stop:
                        self.results[name] = stop.value
                entry[2] = []
        return self.results[name]


CHUNKS = 2
PARTS = 2
LEAD_WINDOWS = ([1, 2, 3, 4, 5], [1, 2, 4, 5, 6], [6, 7, 8], [8, 9, 10])
PAIR_WINDOWS = [3, 5]
SIDE_WINDOWS = [7, 8, 10]
BELOW_WINDOWS = ([9, 10, 11, 13, 15], [10, 11, 12, 14, 15])


def shards(tile_count, col_count, front_diag, front_below, ancestor, owner_cols, rel):
    rows, width = front_diag.shape
    lead = PANELS * width
    steps = lead // rows
    tile_pos = lax.axis_index("tiles")
    col_pos = lax.axis_index("cols")
    target = lax.dynamic_slice_in_dim(owner_cols, col_pos, 1)[0]
    info = jnp.stack((tile_pos, col_pos)).astype(jnp.int32)
    bits = tile_bits(tile_count)
    turned = bits[-2::-1] + [1]
    plan = Plan()
    chunk = width // CHUNKS
    own_parts = {}

    def below_stream(k, order):
        block = front_below[:, k * chunk : (k + 1) * chunk]
        own_parts[k] = []
        pair = yield from climb(block, col_pos, col_count, plan.tie, own_parts[k])
        both = jnp.concatenate(by_panel(pair, col_pos), 1)
        return (yield from fetch_target(both, order, tile_pos, tile_count, target, plan.tie))

    for k, windows in enumerate(BELOW_WINDOWS):
        plan.add(("below", k), below_stream(k, turned if k % 2 else bits), windows)
    plan.run(0)
    pieces = lax.all_to_all(
        front_diag.reshape(tile_count, rows // tile_count, width), "tiles", 0, 0, tiled=True
    )

    lead_pair = {0: []}

    def pair_stream():
        yield from climb(pieces[2:steps], col_pos, col_count, plan.tie, lead_pair[0])

    def lead_stream(i):
        size = (i + 1) * rows
        if i >= 2:
            plan.advance("pair", lead_pair, 0)
            piece = jnp.concatenate(by_panel(lead_pair[0], col_pos), 2)[i - 2 : i - 1, :, :size]
            return (yield from gather_rows(piece, bits, tile_pos, tile_count, plan.tie))
        take = pieces[i : i + 1, :, : min(size, width)]
        pair = yield from climb(take, col_pos, col_count, plan.tie)
        panels = by_panel(pair, col_pos)
        piece = panels[0] if size <= width else jnp.concatenate(panels, 2)[:, :, :size]
        return (yield from gather_rows(piece, bits, tile_pos, tile_count, plan.tie))

    def side_stream():
        pair = yield from climb(pieces[steps:], col_pos, col_count, plan.tie)
        piece = plan.tie(jnp.concatenate(by_panel(pair, col_pos), 2))
        held = lax.all_gather(piece, "tiles")
        yield []
        if piece.shape[1] % 8:
            held = jnp.swapaxes(held, 0, 1).reshape(1, tile_count - steps, rows, lead)
        return held

    plan.add("pair", pair_stream(), PAIR_WINDOWS)
    for i, windows in enumerate(LEAD_WINDOWS):
        plan.add(("lead", i), lead_stream(i), windows)
    plan.add("side", side_stream(), SIDE_WINDOWS)
    flying = []
    for window in range(1, 4):
        flying += plan.run(window)
    plan.run(4)

    factor_rows, inverse_rows = [], []
    window = 5
    blocks = rows // BLOCK
    cuts = sorted({blocks * p // PARTS for p in range(PARTS + 1)})
    for i in range(steps):
        held = plan.finish(("lead", i))
        state = None
        for first, last in zip(cuts[:-1], cuts[1:]):
            plan.run(window)
            state = tile_part(
                i, first, last, rows, bits, info, held, state and state[:3], inverse_rows, flying
            )
            flying = []
            plan.token = state[5]
            window += 1
        window = 5 + PARTS * (i + 1)
        factor_rows.append(state[0])
        inverse_rows.append(tuple(state[3:5]))
    for k in range(CHUNKS):
        plan.advance(("below", k), own_parts, k)
    plan.run(window)
    pairs = [part for pair in inverse_rows for part in pair]
    solves = [
        jax.ShapeDtypeStruct((rows, width), jnp.float32),
        jax.ShapeDtypeStruct((rows, lead), jnp.bfloat16),
        jax.ShapeDtypeStruct((rows, lead), jnp.bfloat16),
        TOKEN,
    ]
    wide = pltpu.VMEM((rows, lead), jnp.float32)
    below = pl.pallas_call(
        functools.partial(below_kernel, steps),
        out_shape=solves,
        in_specs=[SMEM] + [VMEM] * (2 * CHUNKS + len(pairs)),
        out_specs=[VMEM] * 3 + [SMEM],
        scratch_shapes=[wide],
        compiler_params=limit(),
        cost_estimate=cost(20_000_000_000),
    )(info, *[part for k in range(CHUNKS) for part in own_parts[k]], *pairs)
    plan.token = below[3]
    plan.run(window + 1)
    gathered = plan.finish("side")
    sems = pltpu.SemaphoreType.DMA((gathered.shape[0],))
    side = pl.pallas_call(
        functools.partial(side_kernel, steps),
        out_shape=solves,
        in_specs=[SMEM, ANY] + [VMEM] * len(pairs),
        out_specs=[VMEM] * 3 + [SMEM],
        scratch_shapes=[wide, sems],
        compiler_params=limit(),
        cost_estimate=cost(20_000_000_000),
    )(info, gathered, *pairs)
    plan.token = side[3]
    plan.run(window + 2)
    flat = jax.ShapeDtypeStruct((rows, width), jnp.float32)
    factor_below, factor_diag, token = pl.pallas_call(
        functools.partial(change_kernel, steps),
        out_shape=[flat, flat, TOKEN],
        in_specs=[SMEM, ANY] + [VMEM] * (steps + 8),
        out_specs=[VMEM] * 2 + [SMEM],
        scratch_shapes=[pltpu.VMEM((width, lead), jnp.float32), sems],
        compiler_params=limit(),
        cost_estimate=cost(20_000_000_000),
    )(info, gathered, *factor_rows, *below[:3], *side[:3], front_below, front_diag)
    plan.token = token
    plan.run(window + 3)
    target_parts = [part for k in range(CHUNKS) for part in plan.finish(("below", k))]
    row_places = lax.dynamic_slice_in_dim(rel, tile_pos * rows, rows) - tile_pos * rows
    col_places = lax.dynamic_slice_in_dim(rel, target * width, width).reshape(2, rows)
    col_places = col_places - target * width - jnp.array([[0], [rows]], jnp.int32)
    ancestor_out = pl.pallas_call(
        update_kernel,
        out_shape=flat,
        in_specs=[SMEM] + [VMEM] * (5 + 2 * CHUNKS),
        out_specs=VMEM,
        scratch_shapes=[pltpu.VMEM((rows, width), jnp.float32)],
        compiler_params=limit(),
        cost_estimate=cost(10_000_000_000),
    )(info, row_places[None], col_places, below[1], below[2], *target_parts, ancestor)
    return (factor_diag, factor_below, ancestor_out)


def solution(mesh):
    placed = (P("tiles", "cols"), P("tiles", "cols"), P("tiles", "cols"), P(), P())
    return jax.shard_map(
        functools.partial(shards, mesh.shape["tiles"], mesh.shape["cols"]),
        mesh=mesh,
        in_specs=placed,
        out_specs=(P("tiles", "cols"), P("tiles", "cols"), P("tiles", "cols")),
        check_vma=False,
    )
```
